32 devices in a mesh: parts: 2 (over y), row: 4 (over z), col: 2 (over core), dp: 2 (over x).
Axes of the slice: x: 2, y: 2, z: 4, core: 2. Of those that a mesh axis runs over, the one named last changes fastest.
Arguments:
- activations: bfloat16 [1280, 4096], P(('parts', 'dp'), ('row', 'col')), parts along dimension 0, may hold values from -6 to 6
- gradients: bfloat16 [1280, 14336], P(('parts', 'dp'), ('row', 'col')), parts along dimension 0, may hold values from -0.59765625 to 0.59765625
- q_act: bfloat16 [4096, 4096], P(None, ('row', 'col')), may hold values from -0.09375 to 0.09375
- q_grad: bfloat16 [14336, 2, 3584], P(None, 'col', 'row'), may hold values from -0.046875 to 0.046875
- lengths: int32 [4, 3], P(('parts', 'dp')), parts along dimension 0, may hold values from 1 to 160, 320 in all within a row
Outputs:
- correction: float32 [8192, 7168], P(('parts', 'row'), ('col', 'dp')), parts along dimension 0
The draws below stay inside these ranges and needn't reach their ends.
There are 2 independent parts, one for each index of `parts`. The reference program is written for one: setup_inputs(seed, part) draws one part's arguments, and reference() takes and returns one part's arrays. A program takes and returns all parts, laid end to end along the dimension named above; an argument that names none is the same for every part. Nothing has to cross between parts.
Inputs may be any that keep to these rules, and one draw needn't show every extreme that they name: Each row holds the lengths of 3 examples that fill one index of dp's 320 tokens; the longest in each row is 160.
All inputs are finite; a program needn't handle non-finite values.
Results may differ from the reference program's by a relative error of at most 0.0033.
Values may be sent and summed in bfloat16 or wider, within the bound.
No kernel may reach another device: no remote copies, remote signals or barrier semaphores. Data moves between devices by JAX's collectives and lax.ppermute only.
A program may use at most 128 MiB of HBM per device.

```python
import math
import jax
import jax.numpy as jnp
import numpy as np
from jax import lax

D = 4096
FF = 14336
FFW = 7168
TOK_DEV = 320
EX_DEV = 3
MOST = 160
TOKENS = 640
N_COL = 2
N_DP = 2


def level_of(rng, dims, cuts, low, top_value):
    loudness = 1.0
    for position, parts in cuts:
        heights = jax.random.uniform(jax.random.fold_in(jax.random.fold_in(rng, 6), position), (parts,), jnp.float32, low / len(cuts), top_value / len(cuts))
        loudness = loudness * jnp.repeat(jnp.exp(heights), dims[position] // parts).reshape((-1,) + (1,) * (len(dims) - 1 - position))
    return loudness


def split_up(count, total, limit, lean):
    weights = [(1 << 20) // math.isqrt(grade ** lean) + 1 for grade in range(2, count + 1)]
    spare, counts = total - limit - (count - 1), [1] * (count - 1)
    while spare > 0:
        candidates = [i for i in range(count - 1) if counts[i] < limit]
        whole, left = sum([weights[i] for i in candidates]), spare
        for i in candidates:
            extra = min(limit - counts[i], max(1, left * weights[i] // whole), spare)
            counts[i] = counts[i] + extra
            spare = spare - extra
    return np.array([limit] + counts)


def ragged_sizes(key, amount, total, limit, lean):
    if amount == 2:
        one = jax.random.randint(key, (), max(1, total - limit), min(limit, total - 1) + 1)
        return jnp.stack([one, total - one])
    sizes = jnp.asarray(split_up(amount, total, limit, lean), jnp.int32)
    pairs = (amount - 1) // 2
    giver, sink = sizes[1:1 + 2 * pairs:2], sizes[2:2 + 2 * pairs:2]
    slack = jnp.minimum(giver - 1, limit - sink)
    moved = jax.random.randint(jax.random.fold_in(key, 1), (pairs,), 0, 1 << 20) % (slack + 1)
    sizes = sizes.at[1:1 + 2 * pairs:2].set(giver - moved).at[2:2 + 2 * pairs:2].set(sink + moved)
    return sizes[jax.random.permutation(jax.random.fold_in(key, 2), amount)]


def bell_draw(own_key, shape, width, limit, shards=(), kind=jnp.bfloat16):
    entries = width * jax.random.normal(own_key, shape, jnp.float32)
    if shards:
        entries = entries * level_of(own_key, shape, shards, -0.22, 0.18)
    return jnp.clip(entries, -limit, limit).astype(kind)


def setup_inputs(seed: int = 0, part: int = 0) -> dict:
    key_of = jax.random.split(jax.random.key(seed), 6)
    own_keys = jax.random.split(jax.random.fold_in(key_of[5], part), 6)
    activations = bell_draw(own_keys[0], (TOKENS, D), 1.0, 6.0, ((0, 2), (1, 8)))
    gradients = bell_draw(own_keys[1], (TOKENS, FF), 0.1, 0.59765625, ((0, 2), (1, 8)))
    q_act = bell_draw(key_of[2], (D, D), D ** -0.5, 0.09375, ((1, 8),))
    q_grad = bell_draw(key_of[3], (FF, N_COL, FFW // N_COL), FF ** -0.5, 0.046875, ((1, 2), (2, 4)))
    lengths = jax.vmap(lambda own: ragged_sizes(own, EX_DEV, TOK_DEV, MOST, 0))(jax.random.split(own_keys[4], N_DP)).reshape((N_DP, EX_DEV)).astype(jnp.int32)
    return {"activations": activations, "gradients": gradients, "q_act": q_act, "q_grad": q_grad, "lengths": lengths}


def reference(activations, gradients, q_act, q_grad, lengths):
    rotated_act = jnp.dot(activations, q_act, preferred_element_type=jnp.float32).astype(jnp.bfloat16)
    basis_grad = q_grad.reshape(FF, FFW)
    rotated_grad = jnp.dot(gradients, basis_grad, preferred_element_type=jnp.float32).astype(jnp.bfloat16)
    act_blocks = rotated_act.reshape(N_DP, TOK_DEV, D)
    grad_blocks = rotated_grad.reshape(N_DP, TOK_DEV, FFW)

    def block_fold(accumulated, pieces):
        act_block, grad_block, lengths_row = pieces
        endings = jnp.cumsum(lengths_row).astype(jnp.int32)
        beginnings = endings - lengths_row
        positions = jnp.arange(TOK_DEV, dtype=jnp.int32)
        member = ((positions[:, None] >= beginnings[None, :]) & (positions[:, None] < endings[None, :])).astype(act_block.dtype)
        for example in range(EX_DEV):
            masked = act_block * member[:, example:example + 1]
            product = jnp.dot(masked.T, grad_block, preferred_element_type=jnp.float32)
            accumulated = accumulated + product * product
        return accumulated, None

    start_sum = jnp.zeros((D, FFW), jnp.float32)
    summed, _ = lax.scan(block_fold, start_sum, (act_blocks, grad_blocks, lengths))
    return summed / (EX_DEV * N_DP)
```

```python
import functools

import jax
import jax.numpy as jnp
from jax import lax
from jax.experimental import pallas as pl
from jax.experimental.pallas import tpu as pltpu
from jax.sharding import PartitionSpec as P

STEP = 64
VMEM_BYTES = 56 * 1024 * 1024


def span_of(lengths_ref, example):
    begin = 0
    for before in range(example):
        begin = begin + lengths_ref[0, before]
    return begin, begin + lengths_ref[0, example]


def window_start(begin, slack):
    return pl.multiple_of(jnp.minimum(begin // STEP * STEP, slack), STEP)


def mask_kernel(examples, window, lengths_ref, act_ref, out_ref):
    slack = act_ref.shape[0] - window
    for example in range(examples):
        begin, end = span_of(lengths_ref, example)
        start = window_start(begin, slack)
        rows = act_ref[pl.ds(start, window), :]
        token = start + lax.broadcasted_iota(jnp.int32, (window, 1), 0)
        inside = (token >= begin) & (token < end)
        kept = jnp.where(inside, rows.astype(jnp.float32), 0.0)
        out_ref[example] = kept.T.astype(out_ref.dtype)


def masked_windows(rotated, lengths, window):
    tokens, directions = rotated.shape
    examples = lengths.shape[1]
    return pl.pallas_call(
        functools.partial(mask_kernel, examples, window),
        out_shape=jax.ShapeDtypeStruct((examples, directions, window), rotated.dtype),
        in_specs=[
            pl.BlockSpec(memory_space=pltpu.SMEM),
            pl.BlockSpec(memory_space=pltpu.VMEM),
        ],
        out_specs=pl.BlockSpec(memory_space=pltpu.VMEM),
        compiler_params=pltpu.CompilerParams(vmem_limit_bytes=VMEM_BYTES),
        cost_estimate=pl.CostEstimate(
            flops=0, bytes_accessed=2 * tokens * directions * (1 + examples), transcendentals=0
        ),
    )(lengths, rotated)


def square_kernel(blocks, examples, window, total, *refs):
    lengths_refs, act_refs, grad_refs = refs[:blocks], refs[blocks : 2 * blocks], refs[2 * blocks : 3 * blocks]
    out_ref = refs[3 * blocks]
    directions = out_ref.shape[0]
    piece = min(directions, 256)
    for top in range(0, directions, piece):
        acc = None
        for block in range(blocks):
            slack = grad_refs[block].shape[0] - window
            for example in range(examples):
                begin, _ = span_of(lengths_refs[block], example)
                start = window_start(begin, slack)
                product = jnp.dot(
                    act_refs[block][example, top : top + piece, :],
                    grad_refs[block][pl.ds(start, window), :],
                    preferred_element_type=jnp.float32,
                )
                acc = product * product if acc is None else acc + product * product
        out_ref[top : top + piece, :] = acc / total


def squared_sums(lengths, acts, grads, window, total):
    blocks = len(acts)
    examples, directions, _ = acts[0].shape
    tokens, columns = grads[0].shape
    wide = 256 if columns % 256 == 0 else 128
    return pl.pallas_call(
        functools.partial(square_kernel, blocks, examples, window, total),
        out_shape=jax.ShapeDtypeStruct((directions, columns), jnp.float32),
        grid=(columns // wide,),
        in_specs=[pl.BlockSpec(memory_space=pltpu.SMEM)] * blocks
        + [pl.BlockSpec((examples, directions, window), lambda j: (0, 0, 0))] * blocks
        + [pl.BlockSpec((tokens, wide), lambda j: (0, j))] * blocks,
        out_specs=pl.BlockSpec((directions, wide), lambda j: (0, j)),
        compiler_params=pltpu.CompilerParams(vmem_limit_bytes=VMEM_BYTES),
        cost_estimate=pl.CostEstimate(
            flops=2 * blocks * examples * directions * columns * window,
            bytes_accessed=4 * directions * columns + 2 * blocks * tokens * columns,
            transcendentals=0,
        ),
    )(*lengths, *acts, *grads)


def fold_with(basis, section):
    return jnp.dot(section, basis, preferred_element_type=jnp.float32).astype(jnp.bfloat16)


def on_device(activations, gradients, q_act, q_grad, lengths):
    tokens = activations.shape[0]
    n_dp = lax.axis_size("dp")
    total = lengths.shape[1] * n_dp
    window = min(tokens, 256)
    basis_grad = q_grad.reshape(q_grad.shape[0], q_grad.shape[2])

    def shifted(x, k):
        return lax.ppermute(x, "dp", [(i, (i + k) % n_dp) for i in range(n_dp)])

    rotated_g = fold_with(basis_grad, lax.all_gather(gradients, ("row", "col"), axis=1, tiled=True))
    rotated = fold_with(q_act, lax.all_gather(activations, ("row", "col"), axis=1, tiled=True))
    acts, spans = [rotated], [lengths]
    for k in range(1, n_dp):
        acts.append(shifted(rotated, k))
        spans.append(shifted(lengths, k))
    acts = [lax.all_gather(x, "col", axis=1, tiled=True) for x in acts]
    acts = [masked_windows(x, s, window) for x, s in zip(acts, spans)]

    rotated_g = lax.all_gather(rotated_g, "row", axis=1, tiled=True)
    columns = rotated_g.shape[1] // n_dp
    me = lax.axis_index("dp")

    def columns_of(d):
        return lax.dynamic_slice_in_dim(rotated_g, d % n_dp * columns, columns, axis=1)

    grads = [columns_of(me)]
    for k in range(1, n_dp):
        grads.append(shifted(columns_of(me + k), k))
    return squared_sums(spans, acts, grads, window, total)


def solution(mesh):
    return jax.shard_map(
        on_device,
        mesh=mesh,
        in_specs=(
            P(("parts", "dp"), ("row", "col")),
            P(("parts", "dp"), ("row", "col")),
            P(None, ("row", "col")),
            P(None, "col", "row"),
            P(("parts", "dp"), None),
        ),
        out_specs=P(("parts", "row"), ("col", "dp")),
        check_vma=False,
    )
```

```python
import functools

import jax
import jax.numpy as jnp
from jax import lax
from jax.experimental import pallas as pl
from jax.experimental.pallas import tpu as pltpu
from jax.sharding import PartitionSpec as P

STEP = 64
VMEM_BYTES = 56 * 1024 * 1024


def span_of(lengths_ref, example):
    begin = 0
    for before in range(example):
        begin = begin + lengths_ref[0, before]
    return begin, begin + lengths_ref[0, example]


def window_start(begin, slack):
    return pl.multiple_of(jnp.minimum(begin // STEP * STEP, slack), STEP)


def mask_kernel(examples, window, core_ref, lengths_ref, mine_ref, theirs_ref, out_ref):
    slack = mine_ref.shape[0] - window
    half = mine_ref.shape[1]
    for example in range(examples):
        begin, end = span_of(lengths_ref, example)
        start = window_start(begin, slack)
        token = start + lax.broadcasted_iota(jnp.int32, (window, 1), 0)
        inside = (token >= begin) & (token < end)
        for place, ref in ((core_ref[0], mine_ref), (1 - core_ref[0], theirs_ref)):
            rows = ref[pl.ds(start, window), :]
            kept = jnp.where(inside, rows.astype(jnp.float32), 0.0)
            out_ref[example, pl.ds(pl.multiple_of(place * half, half), half), :] = kept.T.astype(out_ref.dtype)


def masked_windows(core, lengths, mine, theirs, window):
    tokens, half = mine.shape
    examples = lengths.shape[1]
    return pl.pallas_call(
        functools.partial(mask_kernel, examples, window),
        name="masked_windows",
        out_shape=jax.ShapeDtypeStruct((examples, 2 * half, window), mine.dtype),
        in_specs=[pl.BlockSpec(memory_space=pltpu.SMEM)] * 2 + [pl.BlockSpec(memory_space=pltpu.VMEM)] * 2,
        out_specs=pl.BlockSpec(memory_space=pltpu.VMEM),
        compiler_params=pltpu.CompilerParams(vmem_limit_bytes=VMEM_BYTES),
    )(core, lengths, mine, theirs)


def square_kernel(chunks, examples, window, total, place_ref, choice_ref, *refs):
    blocks = len(chunks)
    lengths_refs, act_refs, refs = refs[:blocks], refs[blocks : 2 * blocks], refs[2 * blocks :]
    sem, grad_refs, out_ref = refs[-1], refs[-1 - blocks : -1], refs[-2 - blocks]

    @pl.when(pl.program_id(0) == 0)
    def _():
        landed, at, place = [], 0, 0
        for block in range(blocks):
            top = 0
            for rows, arrays in chunks[block]:
                target = grad_refs[block].at[pl.ds(top, rows), :]
                for index in range(arrays):

                    @pl.when(choice_ref[place] == index)
                    def _():
                        pltpu.make_async_copy(refs[at + index], target, sem.at[place]).start()

                landed.append(pltpu.make_async_copy(refs[at], target, sem.at[place]))
                top, at, place = top + rows, at + arrays, place + 1
        for copy in landed:
            copy.wait()

    rows, columns = out_ref.shape
    wide, tall = min(columns, 256), min(rows, 128)
    for left in range(0, columns, wide):
        right = min(left + wide, columns)
        for top in range(0, rows, tall):
            acc = None
            for block in range(blocks):
                slack = grad_refs[block].shape[0] - window
                for example in range(examples):
                    begin, _ = span_of(lengths_refs[block], example)
                    product = jnp.dot(
                        act_refs[block][example, top : top + tall, :],
                        grad_refs[block][pl.ds(window_start(begin, slack), window), left:right],
                        preferred_element_type=jnp.float32,
                    )
                    acc = product * product if acc is None else acc + product * product
            out_ref[top : top + tall, left:right] = acc / total


def squared_sums(lengths, acts, grads, window, total, places=1, place=None, onto=None):
    blocks = len(acts)
    examples, directions, _ = acts[0].shape
    columns = grads[0][0][1][0].shape[1]
    chunks = [[(arrays[0].shape[0], len(arrays)) for _, arrays in block] for block in grads]
    choices = jnp.stack([jnp.asarray(choice, jnp.int32) for block in grads for choice, _ in block])
    flat = [x for block in grads for _, arrays in block for x in arrays]
    tall = min(directions, 512)
    place = jnp.asarray(0 if place is None else place, jnp.int32).reshape(1)
    operands = [choices, *lengths, *acts, *flat]
    in_specs = (
        [pl.BlockSpec(memory_space=pltpu.SMEM)] * (1 + blocks)
        + [pl.BlockSpec((examples, tall, window), lambda i, place: (0, i, 0))] * blocks
        + [pl.BlockSpec(memory_space=pl.ANY)] * len(flat)
    )
    aliases = {}
    if onto is not None:
        aliases = {1 + len(operands): 0}
        operands.append(onto)
        in_specs.append(pl.BlockSpec(memory_space=pl.ANY))
    return pl.pallas_call(
        functools.partial(square_kernel, chunks, examples, window, total),
        name="squared_sums",
        out_shape=jax.ShapeDtypeStruct((directions, places * columns), jnp.float32),
        grid_spec=pltpu.PrefetchScalarGridSpec(
            num_scalar_prefetch=1,
            grid=(directions // tall,),
            in_specs=in_specs,
            out_specs=pl.BlockSpec((tall, columns), lambda i, place: (i, place[0])),
            scratch_shapes=[pltpu.VMEM((sum(rows for rows, _ in c), columns), jnp.bfloat16) for c in chunks]
            + [pltpu.SemaphoreType.DMA((len(choices),))],
        ),
        input_output_aliases=aliases,
        compiler_params=pltpu.CompilerParams(vmem_limit_bytes=VMEM_BYTES),
    )(place, *operands)


def fold_kernel(started, parts, offsets_ref, *refs):
    start_ref = refs[0] if started else None
    mine, theirs = refs[started : started + parts], refs[started + parts : started + 2 * parts]
    basis_ref, *out_refs, sum_ref = refs[started + 2 * parts :]
    step = pl.program_id(0)

    def product(pieces):
        rows = pieces[0][...] if parts == 1 else jnp.concatenate([x[...] for x in pieces], axis=0)
        return jnp.dot(rows, basis_ref[...], preferred_element_type=jnp.float32)

    @pl.when(step == 0)
    def _():
        sum_ref[...] = start_ref[...] + product(mine) if started else product(mine)

    @pl.when(step == 1)
    def _():
        total = sum_ref[...] + product(theirs)
        rows = total.shape[0] // len(out_refs)
        for index, out_ref in enumerate(out_refs):
            out_ref[...] = total[index * rows : index * rows + rows, :].astype(out_ref.dtype)


def fold_block(start, mine, theirs, basis, features, offsets, place, kind, chunks=1):
    tokens = sum(x.shape[0] for x in mine)
    columns = basis.shape[1]
    started = start is not None
    sections = [pl.BlockSpec((x.shape[0], features), lambda i, offsets: (0, 0)) for x in (*mine, *theirs)]
    return pl.pallas_call(
        functools.partial(fold_kernel, started, len(mine)),
        name=f"fold_{place}",
        out_shape=[jax.ShapeDtypeStruct((tokens // chunks, columns), kind)] * chunks,
        grid_spec=pltpu.PrefetchScalarGridSpec(
            num_scalar_prefetch=1,
            grid=(2,),
            in_specs=[pl.BlockSpec((tokens, columns), lambda i, offsets: (0, 0))] * started
            + sections
            + [pl.BlockSpec((features, columns), lambda i, offsets: (offsets[2 * place + i], 0))],
            out_specs=[pl.BlockSpec((tokens // chunks, columns), lambda i, offsets: (0, 0))] * chunks,
            scratch_shapes=[pltpu.VMEM((tokens, columns), jnp.float32)],
        ),
        compiler_params=pltpu.CompilerParams(vmem_limit_bytes=VMEM_BYTES),
    )(offsets, *([start] if started else []), *mine, *theirs, basis)


def project_kernel(steps, offsets_ref, *refs):
    blocks, basis_ref, out_ref, sum_ref = refs[:-3], refs[-3], refs[-2], refs[-1]
    step = pl.program_id(0)
    deep = blocks[0].shape[1]
    total = None
    for place, ref in enumerate(blocks):
        begin = pl.multiple_of((offsets_ref[place] * steps + step) * deep, deep)
        product = jnp.dot(ref[...], basis_ref[pl.ds(begin, deep), :], preferred_element_type=jnp.float32)
        total = product if total is None else total + product

    @pl.when(step == 0)
    def _():
        sum_ref[...] = total

    @pl.when(step > 0)
    def _():
        sum_ref[...] += total

    @pl.when(step == steps - 1)
    def _():
        out_ref[...] = sum_ref[...].astype(out_ref.dtype)


def project(blocks, features, basis, offsets):
    tokens, width = blocks[-1].shape
    columns = basis.shape[1]
    deep = 256
    steps = width // deep

    def tail(x):
        skipped = features // deep if x.shape[1] > width else 0
        return pl.BlockSpec((tokens, deep), lambda i: (0, skipped + i))

    return pl.pallas_call(
        functools.partial(project_kernel, steps),
        name="project",
        out_shape=jax.ShapeDtypeStruct((tokens, columns), basis.dtype),
        grid=(steps,),
        in_specs=[pl.BlockSpec(memory_space=pltpu.SMEM)]
        + [tail(x) for x in blocks]
        + [pl.BlockSpec(basis.shape, lambda i: (0, 0))],
        out_specs=pl.BlockSpec((tokens, columns), lambda i: (0, 0)),
        scratch_shapes=[pltpu.VMEM((tokens, columns), jnp.float32)],
        compiler_params=pltpu.CompilerParams(vmem_limit_bytes=VMEM_BYTES),
    )(offsets, *blocks, basis)


RING = [(0, 1), (1, 3), (3, 2), (2, 0)]


def slots_of(row):
    before = jnp.where(row < 2, 2 - 2 * row, 7 - 2 * row)
    return row, before, 3 - row, 3 - before


def hop(x, what, back=False):
    with jax.named_scope(what):
        return lax.ppermute(x, "row", [hop[::-1] for hop in RING] if back else RING)


def swap(x, axis, what):
    with jax.named_scope(what):
        return lax.ppermute(x, axis, [(0, 1), (1, 0)])


def after(x, *others):
    return lax.optimization_barrier((x, *others))[0]


def chained(activations, gradients, q_act, basis_grad, lengths):
    tokens = activations.shape[0]
    total = 2 * lengths.shape[1]
    window = min(tokens, 256)
    half = tokens // 2
    row, core, me = lax.axis_index("row"), lax.axis_index("col"), lax.axis_index("dp")
    home = row // 2 == me
    outer = (row == 0) | (row == 3)
    cores = core.reshape(1)
    spans = [lengths, swap(lengths, "dp", "lengths_dp")]
    offsets = jnp.stack([2 * s + c for s in slots_of(row) for c in (core, 1 - core)]).astype(jnp.int32)

    features = gradients.shape[1]

    def crossed(chunks, place):
        return [swap(x, "col", f"tokens_{place}_cols_{i}") for i, x in enumerate(chunks)]

    def fold(start, mine, theirs, place):
        return fold_block(start, mine, theirs, basis_grad, features, offsets, place, jnp.float32)[0]

    own = jnp.concatenate([gradients, activations], axis=1)
    slots = [([own], crossed([own], 0))]
    first = hop(own, "tokens_first")
    sums = fold(None, *slots[0], 0)
    second = hop(after(first, sums, spans[1]), "tokens_second")
    slots.append(([first], crossed([first], 1)))
    sums = fold(sums, *slots[1], 1)
    second = after(second, sums)
    third = hop(second[:, :features], "grad_third")
    act_third = hop(second[:, features:], "act_third")
    slots.append(([second], crossed([second], 2)))
    sums = fold(sums, *slots[2], 2)
    third = after(third, sums)
    owns = fold_block(sums, [third], crossed([third], 3), basis_grad, features, offsets, 3, jnp.bfloat16, 2)

    def hops(chunks, what):
        return [hop(x, f"{what}_{i}", i == 1) for i, x in enumerate(chunks)]

    turn = home == outer
    act_third = after(act_third, *owns)
    blocks = [x for mine, theirs in slots for x in (*mine, *theirs)] + [act_third, swap(act_third, "col", "act_third_cols")]
    first = hops(owns, "rot_first")
    rotated = project(blocks, features, q_act, offsets)
    first = after(tuple(first), rotated)
    other = swap(after(rotated, *first), "dp", "act_dp")
    cross_first = swap(jnp.where(turn, first[0], first[1]), "dp", "rot_first_dp")
    second = hops(first, "rot_second")
    second = after(tuple(second), other, cross_first)
    early = [swap(jnp.where(home, s, o), "dp", f"rot_second_dp_{i}") for i, (s, o) in enumerate(zip(second, owns))]
    third = hops(second, "rot_third")
    acts = [(x, swap(x, "col", "rot_act_cols")) for x in (rotated, other)]
    acts = [masked_windows(cores, s, *x, window) for s, x in zip(spans, acts)]
    cross_third = swap(after(jnp.where(turn, third[1], third[0]), *acts, *early), "dp", "rot_third_dp")

    near = [
        [(jnp.where(home, 0, 1), (o, s)) for o, s in zip(owns, second)],
        [(0, (x,)) for x in early],
    ]
    far = [
        [(jnp.where(turn, 1, 0), (first[0], third[0])), (jnp.where(turn, 0, 1), (first[1], third[1]))],
        [(jnp.where(turn, 1, 0), (cross_first, cross_third)), (jnp.where(turn, 0, 1), (cross_first, cross_third))],
    ]
    place = jnp.where(home, row % 2, (3 - row) % 2)
    out = squared_sums(spans, acts, near, window, total, 2, place)
    return squared_sums(spans, acts, far, window, total, 2, 1 - place, out)


def fold_with(basis, section):
    return jnp.dot(section, basis, preferred_element_type=jnp.float32).astype(jnp.bfloat16)


def gathered(activations, gradients, q_act, basis_grad, lengths):
    n_dp = lax.axis_size("dp")
    total = lengths.shape[1] * n_dp
    window = min(activations.shape[0], 256)
    core, me = lax.axis_index("col"), lax.axis_index("dp")
    cores = core.reshape(1)

    def shifted(x, k):
        return lax.ppermute(x, "dp", [(i, (i + k) % n_dp) for i in range(n_dp)])

    rotated_g = fold_with(basis_grad, lax.all_gather(gradients, ("row", "col"), axis=1, tiled=True))
    rotated = fold_with(q_act, lax.all_gather(activations, ("row", "col"), axis=1, tiled=True))
    acts, spans = [rotated], [lengths]
    for k in range(1, n_dp):
        acts.append(shifted(rotated, k))
        spans.append(shifted(lengths, k))
    acts = [masked_windows(cores, s, x, swap(x, "col", "cols"), window) for x, s in zip(acts, spans)]

    rotated_g = lax.all_gather(rotated_g, "row", axis=1, tiled=True)
    columns = rotated_g.shape[1] // n_dp

    def columns_of(d):
        return lax.dynamic_slice_in_dim(rotated_g, d % n_dp * columns, columns, axis=1)

    grads = [columns_of(me)]
    for k in range(1, n_dp):
        grads.append(shifted(columns_of(me + k), k))
    return squared_sums(spans, acts, [[(0, [x])] for x in grads], window, total)


def on_device(activations, gradients, q_act, q_grad, lengths):
    basis_grad = q_grad.reshape(q_grad.shape[0], q_grad.shape[2])
    fits = lax.axis_size("row") == 4 and lax.axis_size("dp") == 2 and lax.axis_size("col") == 2
    plan = chained if fits else gathered
    return plan(activations, gradients, q_act, basis_grad, lengths)


def solution(mesh):
    return jax.shard_map(
        on_device,
        mesh=mesh,
        in_specs=(
            P(("parts", "dp"), ("row", "col")),
            P(("parts", "dp"), ("row", "col")),
            P(None, ("row", "col")),
            P(None, "col", "row"),
            P(("parts", "dp"), None),
        ),
        out_specs=P(("parts", "row"), ("col", "dp")),
        check_vma=False,
    )
```

```python
import functools

import jax
import jax.numpy as jnp
from jax import lax
from jax.experimental import pallas as pl
from jax.experimental.pallas import tpu as pltpu
from jax.sharding import PartitionSpec as P

STEP = 64
VMEM_BYTES = 56 * 1024 * 1024


def span_of(lengths_ref, example):
    begin = 0
    for before in range(example):
        begin = begin + lengths_ref[0, before]
    return begin, begin + lengths_ref[0, example]


def window_start(begin, slack):
    return pl.multiple_of(jnp.minimum(begin // STEP * STEP, slack), STEP)


def mask_kernel(examples, window, place_at, plan_ref, lengths_ref, mine_ref, theirs_ref, out_ref):
    slack = mine_ref.shape[0] - window
    half = mine_ref.shape[1]
    for example in range(examples):
        begin, end = span_of(lengths_ref, example)
        start = window_start(begin, slack)
        token = start + lax.broadcasted_iota(jnp.int32, (window, 1), 0)
        inside = (token >= begin) & (token < end)
        for place, ref in ((plan_ref[place_at], mine_ref), (1 - plan_ref[place_at], theirs_ref)):
            rows = ref[pl.ds(start, window), :]
            kept = jnp.where(inside, rows.astype(jnp.float32), 0.0)
            out_ref[example, pl.ds(pl.multiple_of(place * half, half), half), :] = kept.T.astype(out_ref.dtype)


def masked_windows(plan, place_at, lengths, mine, theirs, window):
    tokens, half = mine.shape
    examples = lengths.shape[1]
    return pl.pallas_call(
        functools.partial(mask_kernel, examples, window, place_at),
        name="masked_windows",
        out_shape=jax.ShapeDtypeStruct((examples, 2 * half, window), mine.dtype),
        in_specs=[pl.BlockSpec(memory_space=pltpu.SMEM)] * 2 + [pl.BlockSpec(memory_space=pltpu.VMEM)] * 2,
        out_specs=pl.BlockSpec(memory_space=pltpu.VMEM),
        compiler_params=pltpu.CompilerParams(vmem_limit_bytes=VMEM_BYTES),
    )(plan, lengths, mine, theirs)


def square_kernel(chunks, examples, window, total, plan_ref, *refs):
    blocks = len(chunks)
    lengths_refs, act_inputs, refs = refs[:blocks], refs[blocks : 2 * blocks], refs[2 * blocks :]
    act_sem, sem, refs = refs[-1], refs[-2], refs[:-2]
    out_ref, grad_refs, act_refs = refs[-2 * blocks - 1], refs[-2 * blocks : -blocks], refs[-blocks:]
    tall = out_ref.shape[0]
    steps = act_refs[0].shape[1] // tall
    now = pl.program_id(0)

    def act_copy(block, step):
        rows = pl.ds(pl.multiple_of(step * tall, tall), tall)
        return pltpu.make_async_copy(act_inputs[block].at[:, rows, :], act_refs[block].at[:, rows, :], act_sem.at[block, step])

    @pl.when(now == 0)
    def _():
        landed, at, place = [], 0, 0
        for block in range(blocks):
            act_copy(block, 0).start()
            top = 0
            for rows, arrays, choice_at in chunks[block]:
                target = grad_refs[block].at[pl.ds(top, rows), :]
                for index in range(arrays):

                    @pl.when((plan_ref[choice_at] == index) | (arrays == 1))
                    def _():
                        pltpu.make_async_copy(refs[at + index], target, sem.at[place]).start()

                landed.append(pltpu.make_async_copy(refs[at], target, sem.at[place]))
                top, at, place = top + rows, at + arrays, place + 1
        for step in range(1, steps):
            for block in range(blocks):
                act_copy(block, step).start()
        for copy in landed:
            copy.wait()

    for block in range(blocks):
        act_copy(block, now).wait()

    rows, columns = out_ref.shape
    wide, high = min(columns, 256), min(rows, 128)
    for left in range(0, columns, wide):
        right = min(left + wide, columns)
        for top in range(0, rows, high):
            acc = None
            for block in range(blocks):
                slack = grad_refs[block].shape[0] - window
                for example in range(examples):
                    begin, _ = span_of(lengths_refs[block], example)
                    product = jnp.dot(
                        act_refs[block][example, pl.ds(pl.multiple_of(now * rows + top, high), high), :],
                        grad_refs[block][pl.ds(window_start(begin, slack), window), left:right],
                        preferred_element_type=jnp.float32,
                    )
                    acc = product * product if acc is None else acc + product * product
            out_ref[top : top + high, left:right] = acc / total


def squared_sums(plan, lengths, acts, grads, window, total, places=1, place_at=0, onto=None):
    blocks = len(acts)
    examples, directions, _ = acts[0].shape
    columns = grads[0][0][1][0].shape[1]
    chunks = [[(arrays[0].shape[0], len(arrays), choice_at) for choice_at, arrays in block] for block in grads]
    flat = [x for block in grads for _, arrays in block for x in arrays]
    tall = min(directions, 512)
    operands = [*lengths, *acts, *flat]
    in_specs = (
        [pl.BlockSpec(memory_space=pltpu.SMEM)] * blocks
        + [pl.BlockSpec(memory_space=pl.ANY)] * (blocks + len(flat))
    )
    aliases = {}
    if onto is not None:
        aliases = {1 + len(operands): 0}
        operands.append(onto)
        in_specs.append(pl.BlockSpec(memory_space=pl.ANY))
    return pl.pallas_call(
        functools.partial(square_kernel, chunks, examples, window, total),
        name="squared_sums",
        out_shape=jax.ShapeDtypeStruct((directions, places * columns), jnp.float32),
        grid_spec=pltpu.PrefetchScalarGridSpec(
            num_scalar_prefetch=1,
            grid=(directions // tall,),
            in_specs=in_specs,
            out_specs=pl.BlockSpec((tall, columns), lambda i, plan: (i, plan[place_at])),
            scratch_shapes=[pltpu.VMEM((sum(c[0] for c in block), columns), jnp.bfloat16) for block in chunks]
            + [pltpu.VMEM(x.shape, x.dtype) for x in acts]
            + [pltpu.SemaphoreType.DMA((sum(len(block) for block in chunks),))]
            + [pltpu.SemaphoreType.DMA((blocks, directions // tall))],
        ),
        input_output_aliases=aliases,
        compiler_params=pltpu.CompilerParams(vmem_limit_bytes=VMEM_BYTES),
    )(plan, *operands)


def fold_kernel(started, parts, offsets_ref, *refs):
    start_ref = refs[0] if started else None
    mine, theirs = refs[started : started + parts], refs[started + parts : started + 2 * parts]
    basis_ref, *out_refs, sum_ref = refs[started + 2 * parts :]
    step = pl.program_id(0)

    def product(pieces):
        rows = pieces[0][...] if parts == 1 else jnp.concatenate([x[...] for x in pieces], axis=0)
        return jnp.dot(rows, basis_ref[...], preferred_element_type=jnp.float32)

    @pl.when(step == 0)
    def _():
        sum_ref[...] = start_ref[...] + product(mine) if started else product(mine)

    @pl.when(step == 1)
    def _():
        total = sum_ref[...] + product(theirs)
        rows = total.shape[0] // len(out_refs)
        for index, out_ref in enumerate(out_refs):
            out_ref[...] = total[index * rows : index * rows + rows, :].astype(out_ref.dtype)


def fold_block(start, mine, theirs, basis, features, offsets, place, kind, chunks=1):
    tokens = sum(x.shape[0] for x in mine)
    columns = basis.shape[1]
    started = start is not None
    sections = [pl.BlockSpec((x.shape[0], features), lambda i, offsets: (0, 0)) for x in (*mine, *theirs)]
    return pl.pallas_call(
        functools.partial(fold_kernel, started, len(mine)),
        name=f"fold_{place}",
        out_shape=[jax.ShapeDtypeStruct((tokens // chunks, columns), kind)] * chunks,
        grid_spec=pltpu.PrefetchScalarGridSpec(
            num_scalar_prefetch=1,
            grid=(2,),
            in_specs=[pl.BlockSpec((tokens, columns), lambda i, offsets: (0, 0))] * started
            + sections
            + [pl.BlockSpec((features, columns), lambda i, offsets: (offsets[2 * place + i], 0))],
            out_specs=[pl.BlockSpec((tokens // chunks, columns), lambda i, offsets: (0, 0))] * chunks,
            scratch_shapes=[pltpu.VMEM((tokens, columns), jnp.float32)],
        ),
        compiler_params=pltpu.CompilerParams(vmem_limit_bytes=VMEM_BYTES),
    )(offsets, *([start] if started else []), *mine, *theirs, basis)


def project_kernel(plan_ref, *refs):
    blocks, basis_ref, out_ref = refs[:-2], refs[-2], refs[-1]
    deep = blocks[0].shape[1]
    total = None
    for place, ref in enumerate(blocks):
        rows = pl.ds(pl.multiple_of(plan_ref[place] * deep, deep), deep)
        product = jnp.dot(ref[...], basis_ref[rows, :], preferred_element_type=jnp.float32)
        total = product if total is None else total + product
    out_ref[...] = total.astype(out_ref.dtype)


def project(blocks, basis, plan):
    return pl.pallas_call(
        project_kernel,
        name="project",
        out_shape=jax.ShapeDtypeStruct((blocks[0].shape[0], basis.shape[1]), basis.dtype),
        in_specs=[pl.BlockSpec(memory_space=pltpu.SMEM)] + [pl.BlockSpec(memory_space=pltpu.VMEM)] * (len(blocks) + 1),
        out_specs=pl.BlockSpec(memory_space=pltpu.VMEM),
        compiler_params=pltpu.CompilerParams(vmem_limit_bytes=VMEM_BYTES),
    )(plan, *blocks, basis)


RING = [(0, 1), (1, 3), (3, 2), (2, 0)]


def slots_of(row):
    before = jnp.where(row < 2, 2 - 2 * row, 7 - 2 * row)
    return row, before, 3 - row, 3 - before


def hop(x, what, back=False):
    with jax.named_scope(what):
        return lax.ppermute(x, "row", [hop[::-1] for hop in RING] if back else RING)


def swap(x, axis, what):
    with jax.named_scope(what):
        return lax.ppermute(x, axis, [(0, 1), (1, 0)])


def after(x, *others):
    return lax.optimization_barrier((x, *others))[0]


def chained(activations, gradients, q_act, basis_grad, lengths):
    tokens = activations.shape[0]
    total = 2 * lengths.shape[1]
    window = min(tokens, 256)
    half = tokens // 2
    row, core, me = lax.axis_index("row"), lax.axis_index("col"), lax.axis_index("dp")
    home = row // 2 == me
    outer = (row == 0) | (row == 3)
    spans = [lengths, swap(lengths, "dp", "lengths_dp")]
    places = [2 * x + c for x in slots_of(row) for c in (core, 1 - core)]
    turn = home == outer
    picks = [jnp.where(home, 0, 1), jnp.where(turn, 1, 0), jnp.where(turn, 0, 1)]
    place = jnp.where(home, row, 3 - row) % 2
    plan = jnp.stack([*places, *picks, place, 1 - place, core]).astype(jnp.int32)
    PICK, TURN, AGAIN, NEAR, FAR, CORE = range(8, 14)

    features = gradients.shape[1]

    def crossed(chunks, place):
        return [swap(x, "col", f"grad_{place}_cols_{i}") for i, x in enumerate(chunks)]

    def fold(start, mine, theirs, place):
        return fold_block(start, mine, theirs, basis_grad, features, plan, place, jnp.float32)[0]

    def piece(sums, x, place, i):
        theirs = swap(x, "col", f"grad_{place}_cols_{i}")
        kind = jnp.bfloat16 if place == 3 else jnp.float32
        return fold_block(sums, [x], [theirs], basis_grad, features, plan, place, kind)[0]

    own = [gradients[i : i + half] for i in (0, half)]
    sums = list(fold_block(None, own, crossed(own, 0), basis_grad, features, plan, 0, jnp.float32, 2))
    firsts = [after(hop(x, f"grad_first_{i}"), sums[i], spans[1]) for i, x in enumerate(own)]
    act_first = hop(after(activations, *sums), "act_first")
    seconds = [hop(after(x, act_first) if 0 else x, f"grad_second_{i}") for i, x in enumerate(firsts)]
    act_second = hop(act_first, "act_second")
    act_third = hop(act_second, "act_third")
    thirds = []
    for i in range(2):
        sums[i] = piece(sums[i], firsts[i], 1, i)
        thirds.append(hop(after(seconds[i], sums[i], *([act_second] if i else [])), f"grad_third_{i}"))
    sums[1] = piece(sums[1], seconds[1], 2, 1)
    acts = (activations, act_first, act_second, act_third)
    rotated = project([x for s in acts for x in (s, swap(s, "col", "act_cols"))], q_act, plan)
    other = swap(rotated, "dp", "act_dp")
    acts = [(x, swap(x, "col", "rot_act_cols")) for x in (rotated, other)]
    owns = [None, piece(sums[1], after(thirds[1], sums[1], rotated), 3, 1)]
    sums[0] = piece(after(sums[0], owns[1]) if 0 else sums[0], seconds[0], 2, 0)
    owns[0] = piece(sums[0], after(thirds[0], sums[0], owns[1], *acts[1]), 3, 0)

    acts = [masked_windows(plan, CORE, s, *x, window) for s, x in zip(spans, acts)]
    first = [hop(x, f"rot_first_{i}", i == 1) for i, x in enumerate(owns)]
    second = [None, hop(after(first[1], owns[0]), "rot_second_1", True)]
    second[0] = hop(first[0], "rot_second_0")
    cross_first = swap(jnp.where(turn, first[0], first[1]), "dp", "rot_first_dp")
    early = [jnp.where(home, s, o) for s, o in zip(second, owns)]
    early[1] = swap(early[1], "dp", "rot_second_dp_1")
    third = [None, hop(second[1], "rot_third_1", True)]
    third[0] = hop(after(second[0], third[1], cross_first, early[1]), "rot_third_0")
    early[0] = swap(early[0], "dp", "rot_second_dp_0")
    cross_third = jnp.where(turn, third[1], third[0])
    cross_third = swap(after(cross_third, *early, *acts), "dp", "rot_third_dp")

    near = [[(PICK, (o, s)) for o, s in zip(owns, second)], [(PICK, (x,)) for x in early]]
    far = [[(TURN, (first[0], third[0])), (AGAIN, (first[1], third[1]))], [(at, (cross_first, cross_third)) for at in (TURN, AGAIN)]]
    out = squared_sums(plan, spans, acts, near, window, total, 2, NEAR)
    return squared_sums(plan, spans, acts, far, window, total, 2, FAR, out)


def fold_with(basis, section):
    return jnp.dot(section, basis, preferred_element_type=jnp.float32).astype(jnp.bfloat16)


def gathered(activations, gradients, q_act, basis_grad, lengths):
    n_dp = lax.axis_size("dp")
    total = lengths.shape[1] * n_dp
    window = min(activations.shape[0], 256)
    me = lax.axis_index("dp")
    plan = jnp.stack([jnp.int32(0), lax.axis_index("col").astype(jnp.int32)])

    def shifted(x, k):
        return lax.ppermute(x, "dp", [(i, (i + k) % n_dp) for i in range(n_dp)])

    rotated_g = fold_with(basis_grad, lax.all_gather(gradients, ("row", "col"), axis=1, tiled=True))
    rotated = fold_with(q_act, lax.all_gather(activations, ("row", "col"), axis=1, tiled=True))
    acts, spans = [rotated], [lengths]
    for k in range(1, n_dp):
        acts.append(shifted(rotated, k))
        spans.append(shifted(lengths, k))
    acts = [masked_windows(plan, 1, s, x, swap(x, "col", "cols"), window) for x, s in zip(acts, spans)]

    rotated_g = lax.all_gather(rotated_g, "row", axis=1, tiled=True)
    columns = rotated_g.shape[1] // n_dp

    def columns_of(d):
        return lax.dynamic_slice_in_dim(rotated_g, d % n_dp * columns, columns, axis=1)

    grads = [columns_of(me)]
    for k in range(1, n_dp):
        grads.append(shifted(columns_of(me + k), k))
    return squared_sums(plan, spans, acts, [[(0, [x])] for x in grads], window, total)


def on_device(activations, gradients, q_act, q_grad, lengths):
    basis_grad = q_grad.reshape(q_grad.shape[0], q_grad.shape[2])
    fits = lax.axis_size("row") == 4 and lax.axis_size("dp") == 2 and lax.axis_size("col") == 2
    plan = chained if fits else gathered
    return plan(activations, gradients, q_act, basis_grad, lengths)


def solution(mesh):
    return jax.shard_map(
        on_device,
        mesh=mesh,
        in_specs=(
            P(("parts", "dp"), ("row", "col")),
            P(("parts", "dp"), ("row", "col")),
            P(None, ("row", "col")),
            P(None, "col", "row"),
            P(("parts", "dp"), None),
        ),
        out_specs=P(("parts", "row"), ("col", "dp")),
        check_vma=False,
    )
```

```python
import functools

import jax
import jax.numpy as jnp
from jax import lax
from jax.experimental import pallas as pl
from jax.experimental.pallas import tpu as pltpu
from jax.sharding import PartitionSpec as P

STEP = 64
VMEM_BYTES = 40 * 1024 * 1024


def span_of(lengths_ref, example):
    begin = 0
    for before in range(example):
        begin = begin + lengths_ref[0, before]
    return begin, begin + lengths_ref[0, example]


def window_start(begin, slack):
    return pl.multiple_of(jnp.minimum(begin // STEP * STEP, slack), STEP)


def mask_kernel(examples, window, place_at, plan_ref, lengths_ref, mine_ref, theirs_ref, out_ref):
    slack = mine_ref.shape[0] - window
    half = mine_ref.shape[1]
    for example in range(examples):
        begin, end = span_of(lengths_ref, example)
        start = window_start(begin, slack)
        token = start + lax.broadcasted_iota(jnp.int32, (window, 1), 0)
        inside = (token >= begin) & (token < end)
        for place, ref in ((plan_ref[place_at], mine_ref), (1 - plan_ref[place_at], theirs_ref)):
            rows = ref[pl.ds(start, window), :]
            kept = jnp.where(inside, rows.astype(jnp.float32), 0.0)
            out_ref[example, pl.ds(pl.multiple_of(place * half, half), half), :] = kept.T.astype(out_ref.dtype)


def masked_windows(plan, place_at, lengths, mine, theirs, window):
    tokens, half = mine.shape
    examples = lengths.shape[1]
    return pl.pallas_call(
        functools.partial(mask_kernel, examples, window, place_at),
        name="masked_windows",
        out_shape=jax.ShapeDtypeStruct((examples, 2 * half, window), mine.dtype),
        in_specs=[pl.BlockSpec(memory_space=pltpu.SMEM)] * 2 + [pl.BlockSpec(memory_space=pltpu.VMEM)] * 2,
        out_specs=pl.BlockSpec(memory_space=pltpu.VMEM),
        compiler_params=pltpu.CompilerParams(vmem_limit_bytes=VMEM_BYTES),
    )(plan, lengths, mine, theirs)


def square_kernel(chunks, examples, window, total, plan_ref, *refs):
    blocks = len(chunks)
    lengths_refs, act_inputs, refs = refs[:blocks], refs[blocks : 2 * blocks], refs[2 * blocks :]
    act_sem, sem, refs = refs[-1], refs[-2], refs[:-2]
    out_ref, grad_refs, act_refs = refs[-2 * blocks - 1], refs[-2 * blocks : -blocks], refs[-blocks:]
    tall = out_ref.shape[0]
    steps = act_refs[0].shape[1] // tall
    now = pl.program_id(0)

    def act_copy(block, step):
        rows = pl.ds(pl.multiple_of(step * tall, tall), tall)
        return pltpu.make_async_copy(act_inputs[block].at[:, rows, :], act_refs[block].at[:, rows, :], act_sem.at[block, step])

    @pl.when(now == 0)
    def _():
        landed, at, place = [], 0, 0
        for block in range(blocks):
            act_copy(block, 0).start()
            top = 0
            for rows, arrays, choice_at in chunks[block]:
                target = grad_refs[block].at[pl.ds(top, rows), :]
                for index in range(arrays):

                    @pl.when((plan_ref[choice_at] == index) | (arrays == 1))
                    def _():
                        pltpu.make_async_copy(refs[at + index], target, sem.at[place]).start()

                landed.append(pltpu.make_async_copy(refs[at], target, sem.at[place]))
                top, at, place = top + rows, at + arrays, place + 1
        for step in range(1, steps):
            for block in range(blocks):
                act_copy(block, step).start()
        for copy in landed:
            copy.wait()

    for block in range(blocks):
        act_copy(block, now).wait()

    rows, columns = out_ref.shape
    wide, high = min(columns, 256), min(rows, 128)
    for left in range(0, columns, wide):
        right = min(left + wide, columns)
        for top in range(0, rows, high):
            acc = None
            for block in range(blocks):
                slack = grad_refs[block].shape[0] - window
                for example in range(examples):
                    begin, _ = span_of(lengths_refs[block], example)
                    product = jnp.dot(
                        act_refs[block][example, pl.ds(pl.multiple_of(now * rows + top, high), high), :],
                        grad_refs[block][pl.ds(window_start(begin, slack), window), left:right],
                        preferred_element_type=jnp.float32,
                    )
                    acc = product * product if acc is None else acc + product * product
            out_ref[top : top + high, left:right] = acc / total


def squared_sums(plan, lengths, acts, grads, window, total, places=1, place_at=0, onto=None):
    blocks = len(acts)
    examples, directions, _ = acts[0].shape
    columns = grads[0][0][1][0].shape[1]
    chunks = [[(arrays[0].shape[0], len(arrays), choice_at) for choice_at, arrays in block] for block in grads]
    flat = [x for block in grads for _, arrays in block for x in arrays]
    tall = min(directions, 512)
    operands = [*lengths, *acts, *flat]
    in_specs = (
        [pl.BlockSpec(memory_space=pltpu.SMEM)] * blocks
        + [pl.BlockSpec(memory_space=pl.ANY)] * (blocks + len(flat))
    )
    aliases = {}
    if onto is not None:
        aliases = {1 + len(operands): 0}
        operands.append(onto)
        in_specs.append(pl.BlockSpec(memory_space=pl.ANY))
    return pl.pallas_call(
        functools.partial(square_kernel, chunks, examples, window, total),
        name="squared_sums",
        out_shape=jax.ShapeDtypeStruct((directions, places * columns), jnp.float32),
        grid_spec=pltpu.PrefetchScalarGridSpec(
            num_scalar_prefetch=1,
            grid=(directions // tall,),
            in_specs=in_specs,
            out_specs=pl.BlockSpec((tall, columns), lambda i, plan: (i, plan[place_at])),
            scratch_shapes=[pltpu.VMEM((sum(c[0] for c in block), columns), jnp.bfloat16) for block in chunks]
            + [pltpu.VMEM(x.shape, x.dtype) for x in acts]
            + [pltpu.SemaphoreType.DMA((sum(len(block) for block in chunks),))]
            + [pltpu.SemaphoreType.DMA((blocks, directions // tall))],
        ),
        input_output_aliases=aliases,
        compiler_params=pltpu.CompilerParams(vmem_limit_bytes=VMEM_BYTES),
    )(plan, *operands)


def fold_kernel(started, parts, offsets_ref, *refs):
    start_ref = refs[0] if started else None
    mine, theirs = refs[started : started + parts], refs[started + parts : started + 2 * parts]
    basis_ref, *out_refs, sum_ref = refs[started + 2 * parts :]
    step = pl.program_id(0)

    def product(pieces):
        rows = pieces[0][...] if parts == 1 else jnp.concatenate([x[...] for x in pieces], axis=0)
        return jnp.dot(rows, basis_ref[...], preferred_element_type=jnp.float32)

    @pl.when(step == 0)
    def _():
        sum_ref[...] = start_ref[...] + product(mine) if started else product(mine)

    @pl.when(step == 1)
    def _():
        total = sum_ref[...] + product(theirs)
        rows = total.shape[0] // len(out_refs)
        for index, out_ref in enumerate(out_refs):
            out_ref[...] = total[index * rows : index * rows + rows, :].astype(out_ref.dtype)


def fold_block(start, mine, theirs, basis, features, offsets, place, kind, chunks=1):
    tokens = sum(x.shape[0] for x in mine)
    columns = basis.shape[1]
    started = start is not None
    sections = [pl.BlockSpec((x.shape[0], features), lambda i, offsets: (0, 0)) for x in (*mine, *theirs)]
    return pl.pallas_call(
        functools.partial(fold_kernel, started, len(mine)),
        name=f"fold_{place}",
        out_shape=[jax.ShapeDtypeStruct((tokens // chunks, columns), kind)] * chunks,
        grid_spec=pltpu.PrefetchScalarGridSpec(
            num_scalar_prefetch=1,
            grid=(2,),
            in_specs=[pl.BlockSpec((tokens, columns), lambda i, offsets: (0, 0))] * started
            + sections
            + [pl.BlockSpec((features, columns), lambda i, offsets: (offsets[2 * place + i], 0))],
            out_specs=[pl.BlockSpec((tokens // chunks, columns), lambda i, offsets: (0, 0))] * chunks,
            scratch_shapes=[pltpu.VMEM((tokens, columns), jnp.float32)],
        ),
        compiler_params=pltpu.CompilerParams(vmem_limit_bytes=VMEM_BYTES),
    )(offsets, *([start] if started else []), *mine, *theirs, basis)


def project_kernel(plan_ref, *refs):
    blocks, basis_ref, out_ref = refs[:-2], refs[-2], refs[-1]
    deep = blocks[0].shape[1]
    total = None
    for place, ref in enumerate(blocks):
        rows = pl.ds(pl.multiple_of(plan_ref[place] * deep, deep), deep)
        product = jnp.dot(ref[...], basis_ref[rows, :], preferred_element_type=jnp.float32)
        total = product if total is None else total + product
    out_ref[...] = total.astype(out_ref.dtype)


def project(blocks, basis, plan):
    return pl.pallas_call(
        project_kernel,
        name="project",
        out_shape=jax.ShapeDtypeStruct((blocks[0].shape[0], basis.shape[1]), basis.dtype),
        in_specs=[pl.BlockSpec(memory_space=pltpu.SMEM)] + [pl.BlockSpec(memory_space=pltpu.VMEM)] * (len(blocks) + 1),
        out_specs=pl.BlockSpec(memory_space=pltpu.VMEM),
        compiler_params=pltpu.CompilerParams(vmem_limit_bytes=VMEM_BYTES),
    )(plan, *blocks, basis)


RING = [(0, 1), (1, 3), (3, 2), (2, 0)]


def slots_of(row):
    before = jnp.where(row < 2, 2 - 2 * row, 7 - 2 * row)
    return row, before, 3 - row, 3 - before


def hop(x, what, back=False):
    with jax.named_scope(what):
        return lax.ppermute(x, "row", [hop[::-1] for hop in RING] if back else RING)


def swap(x, axis, what):
    with jax.named_scope(what):
        return lax.ppermute(x, axis, [(0, 1), (1, 0)])


def after(x, *others):
    return lax.optimization_barrier((x, *others))[0]


def chained(activations, gradients, q_act, basis_grad, lengths):
    tokens = activations.shape[0]
    total = 2 * lengths.shape[1]
    window = min(tokens, 256)
    half = tokens // 2
    row, core, me = lax.axis_index("row"), lax.axis_index("col"), lax.axis_index("dp")
    home = row // 2 == me
    outer = (row == 0) | (row == 3)
    spans = [lengths, swap(lengths, "dp", "lengths_dp")]
    places = [2 * x + c for x in slots_of(row) for c in (core, 1 - core)]
    turn = home == outer
    picks = [jnp.where(home, 0, 1), jnp.where(turn, 1, 0), jnp.where(turn, 0, 1)]
    place = jnp.where(home, row, 3 - row) % 2
    plan = jnp.stack([*places, *picks, place, 1 - place, core]).astype(jnp.int32)
    PICK, TURN, AGAIN, NEAR, FAR, CORE = range(8, 14)

    features = gradients.shape[1]

    def crossed(chunks, place):
        return [swap(x, "col", f"grad_{place}_cols_{i}") for i, x in enumerate(chunks)]

    def fold(start, mine, theirs, place):
        return fold_block(start, mine, theirs, basis_grad, features, plan, place, jnp.float32)[0]

    def piece(sums, x, place, i):
        theirs = swap(x, "col", f"grad_{place}_cols_{i}")
        kind = jnp.bfloat16 if place == 3 else jnp.float32
        return fold_block(sums, [x], [theirs], basis_grad, features, plan, place, kind)[0]

    own = [gradients[i : i + half] for i in (0, half)]
    sums = list(fold_block(None, own, crossed(own, 0), basis_grad, features, plan, 0, jnp.float32, 2))
    firsts = [after(hop(x, f"grad_first_{i}"), sums[i], spans[1]) for i, x in enumerate(own)]
    act_first = hop(after(activations, *sums), "act_first")
    seconds = [hop(x, f"grad_second_{i}") for i, x in enumerate(firsts)]
    act_second = hop(act_first, "act_second")
    thirds = [None, None]
    sums[1] = piece(sums[1], firsts[1], 1, 1)
    act_third = hop(after(act_second, sums[1]), "act_third")
    sums[0] = piece(sums[0], firsts[0], 1, 0)
    thirds[1] = hop(after(seconds[1], sums[1], act_second), "grad_third_1")
    thirds[0] = hop(after(seconds[0], sums[0]), "grad_third_0")
    acts = (activations, act_first, act_second, act_third)
    rotated = project([x for s in acts for x in (s, swap(s, "col", "act_cols"))], q_act, plan)
    other = swap(rotated, "dp", "act_dp")
    acts = [(x, swap(x, "col", "rot_act_cols")) for x in (rotated, other)]
    sums[1] = piece(sums[1], seconds[1], 2, 1)
    owns = [None, piece(sums[1], after(thirds[1], sums[1], rotated), 3, 1)]
    sums[0] = piece(sums[0], seconds[0], 2, 0)
    owns[0] = piece(sums[0], after(thirds[0], sums[0], owns[1], *acts[1]), 3, 0)

    acts = [masked_windows(plan, CORE, s, *x, window) for s, x in zip(spans, acts)]
    first = [hop(x, f"rot_first_{i}", i == 1) for i, x in enumerate(owns)]
    second = [None, hop(after(first[1], owns[0]), "rot_second_1", True)]
    second[0] = hop(first[0], "rot_second_0")
    cross_first = swap(jnp.where(turn, first[0], first[1]), "dp", "rot_first_dp")
    early = [jnp.where(home, s, o) for s, o in zip(second, owns)]
    early[1] = swap(early[1], "dp", "rot_second_dp_1")
    third = [None, hop(second[1], "rot_third_1", True)]
    third[0] = hop(after(second[0], third[1], cross_first, early[1]), "rot_third_0")
    early[0] = swap(early[0], "dp", "rot_second_dp_0")
    cross_third = jnp.where(turn, third[1], third[0])
    cross_third = swap(after(cross_third, *early, *acts), "dp", "rot_third_dp")

    near = [[(PICK, (o, s)) for o, s in zip(owns, second)], [(PICK, (x,)) for x in early]]
    far = [[(TURN, (first[0], third[0])), (AGAIN, (first[1], third[1]))], [(at, (cross_first, cross_third)) for at in (TURN, AGAIN)]]
    out = squared_sums(plan, spans, acts, near, window, total, 2, NEAR)
    return squared_sums(plan, spans, acts, far, window, total, 2, FAR, out)


def fold_with(basis, section):
    return jnp.dot(section, basis, preferred_element_type=jnp.float32).astype(jnp.bfloat16)


def gathered(activations, gradients, q_act, basis_grad, lengths):
    n_dp = lax.axis_size("dp")
    total = lengths.shape[1] * n_dp
    window = min(activations.shape[0], 256)
    me = lax.axis_index("dp")
    plan = jnp.stack([jnp.int32(0), lax.axis_index("col").astype(jnp.int32)])

    def shifted(x, k):
        return lax.ppermute(x, "dp", [(i, (i + k) % n_dp) for i in range(n_dp)])

    rotated_g = fold_with(basis_grad, lax.all_gather(gradients, ("row", "col"), axis=1, tiled=True))
    rotated = fold_with(q_act, lax.all_gather(activations, ("row", "col"), axis=1, tiled=True))
    acts, spans = [rotated], [lengths]
    for k in range(1, n_dp):
        acts.append(shifted(rotated, k))
        spans.append(shifted(lengths, k))
    acts = [masked_windows(plan, 1, s, x, swap(x, "col", "cols"), window) for x, s in zip(acts, spans)]

    rotated_g = lax.all_gather(rotated_g, "row", axis=1, tiled=True)
    columns = rotated_g.shape[1] // n_dp

    def columns_of(d):
        return lax.dynamic_slice_in_dim(rotated_g, d % n_dp * columns, columns, axis=1)

    grads = [columns_of(me)]
    for k in range(1, n_dp):
        grads.append(shifted(columns_of(me + k), k))
    return squared_sums(plan, spans, acts, [[(0, [x])] for x in grads], window, total)


def on_device(activations, gradients, q_act, q_grad, lengths):
    basis_grad = q_grad.reshape(q_grad.shape[0], q_grad.shape[2])
    fits = lax.axis_size("row") == 4 and lax.axis_size("dp") == 2 and lax.axis_size("col") == 2
    plan = chained if fits else gathered
    return plan(activations, gradients, q_act, basis_grad, lengths)


def solution(mesh):
    return jax.shard_map(
        on_device,
        mesh=mesh,
        in_specs=(
            P(("parts", "dp"), ("row", "col")),
            P(("parts", "dp"), ("row", "col")),
            P(None, ("row", "col")),
            P(None, "col", "row"),
            P(("parts", "dp"), None),
        ),
        out_specs=P(("parts", "row"), ("col", "dp")),
        check_vma=False,
    )
```

```python
import functools

import jax
import jax.numpy as jnp
from jax import lax
from jax.experimental import pallas as pl
from jax.experimental.pallas import tpu as pltpu
from jax.sharding import PartitionSpec as P

STEP = 64
VMEM_BYTES = 40 * 1024 * 1024


def span_of(lengths_ref, example):
    begin = 0
    for before in range(example):
        begin = begin + lengths_ref[0, before]
    return begin, begin + lengths_ref[0, example]


def window_start(begin, slack):
    return pl.multiple_of(jnp.minimum(begin // STEP * STEP, slack), STEP)


def mask_kernel(examples, window, place_at, plan_ref, lengths_ref, mine_ref, theirs_ref, out_ref):
    slack = mine_ref.shape[0] - window
    half = mine_ref.shape[1]
    for example in range(examples):
        begin, end = span_of(lengths_ref, example)
        start = window_start(begin, slack)
        token = start + lax.broadcasted_iota(jnp.int32, (window, 1), 0)
        inside = (token >= begin) & (token < end)
        for place, ref in ((plan_ref[place_at], mine_ref), (1 - plan_ref[place_at], theirs_ref)):
            rows = ref[pl.ds(start, window), :]
            kept = jnp.where(inside, rows.astype(jnp.float32), 0.0)
            out_ref[example, pl.ds(pl.multiple_of(place * half, half), half), :] = kept.T.astype(out_ref.dtype)


def masked_windows(plan, place_at, lengths, mine, theirs, window):
    tokens, half = mine.shape
    examples = lengths.shape[1]
    return pl.pallas_call(
        functools.partial(mask_kernel, examples, window, place_at),
        name="masked_windows",
        out_shape=jax.ShapeDtypeStruct((examples, 2 * half, window), mine.dtype),
        in_specs=[pl.BlockSpec(memory_space=pltpu.SMEM)] * 2 + [pl.BlockSpec(memory_space=pltpu.VMEM)] * 2,
        out_specs=pl.BlockSpec(memory_space=pltpu.VMEM),
        compiler_params=pltpu.CompilerParams(vmem_limit_bytes=VMEM_BYTES),
    )(plan, lengths, mine, theirs)


def square_kernel(chunks, examples, window, total, plan_ref, *refs):
    blocks = len(chunks)
    lengths_refs, act_inputs, refs = refs[:blocks], refs[blocks : 2 * blocks], refs[2 * blocks :]
    act_sem, sem, refs = refs[-1], refs[-2], refs[:-2]
    out_ref, grad_refs, act_refs = refs[-2 * blocks - 1], refs[-2 * blocks : -blocks], refs[-blocks:]
    tall = out_ref.shape[0]
    steps = act_refs[0].shape[1] // tall
    now = pl.program_id(0)

    def act_copy(block, step):
        rows = pl.ds(pl.multiple_of(step * tall, tall), tall)
        return pltpu.make_async_copy(act_inputs[block].at[:, rows, :], act_refs[block].at[:, rows, :], act_sem.at[block, step])

    @pl.when(now == 0)
    def _():
        landed, at, place = [], 0, 0
        for block in range(blocks):
            act_copy(block, 0).start()
            top = 0
            for rows, arrays, choice_at in chunks[block]:
                target = grad_refs[block].at[pl.ds(top, rows), :]
                for index in range(arrays):

                    @pl.when((plan_ref[choice_at] == index) | (arrays == 1))
                    def _():
                        pltpu.make_async_copy(refs[at + index], target, sem.at[place]).start()

                landed.append(pltpu.make_async_copy(refs[at], target, sem.at[place]))
                top, at, place = top + rows, at + arrays, place + 1
        for step in range(1, steps):
            for block in range(blocks):
                act_copy(block, step).start()
        for copy in landed:
            copy.wait()

    for block in range(blocks):
        act_copy(block, now).wait()

    rows, columns = out_ref.shape
    wide, high = min(columns, 256), min(rows, 256)
    for left in range(0, columns, wide):
        right = min(left + wide, columns)
        for top in range(0, rows, high):
            acc = None
            for block in range(blocks):
                slack = grad_refs[block].shape[0] - window
                for example in range(examples):
                    begin, _ = span_of(lengths_refs[block], example)
                    product = jnp.dot(
                        act_refs[block][example, pl.ds(pl.multiple_of(now * rows + top, high), high), :],
                        grad_refs[block][pl.ds(window_start(begin, slack), window), left:right],
                        preferred_element_type=jnp.float32,
                    )
                    acc = product * product if acc is None else acc + product * product
            out_ref[top : top + high, left:right] = acc / total


def squared_sums(plan, lengths, acts, grads, window, total, places=1, place_at=0, onto=None):
    blocks = len(acts)
    examples, directions, _ = acts[0].shape
    columns = grads[0][0][1][0].shape[1]
    chunks = [[(arrays[0].shape[0], len(arrays), choice_at) for choice_at, arrays in block] for block in grads]
    flat = [x for block in grads for _, arrays in block for x in arrays]
    tall = min(directions, 512)
    operands = [*lengths, *acts, *flat]
    in_specs = (
        [pl.BlockSpec(memory_space=pltpu.SMEM)] * blocks
        + [pl.BlockSpec(memory_space=pl.ANY)] * (blocks + len(flat))
    )
    aliases = {}
    if onto is not None:
        aliases = {1 + len(operands): 0}
        operands.append(onto)
        in_specs.append(pl.BlockSpec(memory_space=pl.ANY))
    return pl.pallas_call(
        functools.partial(square_kernel, chunks, examples, window, total),
        name="squared_sums",
        out_shape=jax.ShapeDtypeStruct((directions, places * columns), jnp.float32),
        grid_spec=pltpu.PrefetchScalarGridSpec(
            num_scalar_prefetch=1,
            grid=(directions // tall,),
            in_specs=in_specs,
            out_specs=pl.BlockSpec((tall, columns), lambda i, plan: (i, plan[place_at])),
            scratch_shapes=[pltpu.VMEM((sum(c[0] for c in block), columns), jnp.bfloat16) for block in chunks]
            + [pltpu.VMEM(x.shape, x.dtype) for x in acts]
            + [pltpu.SemaphoreType.DMA((sum(len(block) for block in chunks),))]
            + [pltpu.SemaphoreType.DMA((blocks, directions // tall))],
        ),
        input_output_aliases=aliases,
        compiler_params=pltpu.CompilerParams(vmem_limit_bytes=VMEM_BYTES),
    )(plan, *operands)


def fold_kernel(started, parts, offsets_ref, *refs):
    start_ref = refs[0] if started else None
    mine, theirs = refs[started : started + parts], refs[started + parts : started + 2 * parts]
    basis_ref, *out_refs, sum_ref = refs[started + 2 * parts :]
    step = pl.program_id(0)

    def product(pieces):
        rows = pieces[0][...] if parts == 1 else jnp.concatenate([x[...] for x in pieces], axis=0)
        return jnp.dot(rows, basis_ref[...], preferred_element_type=jnp.float32)

    @pl.when(step == 0)
    def _():
        sum_ref[...] = start_ref[...] + product(mine) if started else product(mine)

    @pl.when(step == 1)
    def _():
        total = sum_ref[...] + product(theirs)
        rows = total.shape[0] // len(out_refs)
        for index, out_ref in enumerate(out_refs):
            out_ref[...] = total[index * rows : index * rows + rows, :].astype(out_ref.dtype)


def fold_block(start, mine, theirs, basis, features, offsets, place, kind, chunks=1):
    tokens = sum(x.shape[0] for x in mine)
    columns = basis.shape[1]
    started = start is not None
    sections = [pl.BlockSpec((x.shape[0], features), lambda i, offsets: (0, 0)) for x in (*mine, *theirs)]
    return pl.pallas_call(
        functools.partial(fold_kernel, started, len(mine)),
        name=f"fold_{place}",
        out_shape=[jax.ShapeDtypeStruct((tokens // chunks, columns), kind)] * chunks,
        grid_spec=pltpu.PrefetchScalarGridSpec(
            num_scalar_prefetch=1,
            grid=(2,),
            in_specs=[pl.BlockSpec((tokens, columns), lambda i, offsets: (0, 0))] * started
            + sections
            + [pl.BlockSpec((features, columns), lambda i, offsets: (offsets[2 * place + i], 0))],
            out_specs=[pl.BlockSpec((tokens // chunks, columns), lambda i, offsets: (0, 0))] * chunks,
            scratch_shapes=[pltpu.VMEM((tokens, columns), jnp.float32)],
        ),
        compiler_params=pltpu.CompilerParams(vmem_limit_bytes=VMEM_BYTES),
    )(offsets, *([start] if started else []), *mine, *theirs, basis)


def project_kernel(tops, steps, offsets_ref, *refs):
    blocks, basis_ref, out_ref, sum_ref = refs[:-3], refs[-3], refs[-2], refs[-1]
    step = pl.program_id(0)
    deep = blocks[0].shape[1]

    @pl.when(step == 0)
    def _():
        sum_ref[...] = jnp.zeros_like(sum_ref)

    for ref, (top, place) in zip(blocks, tops):
        begin = pl.multiple_of((offsets_ref[place] * steps + step) * deep, deep)
        sum_ref[top : top + ref.shape[0], :] += jnp.dot(
            ref[...], basis_ref[pl.ds(begin, deep), :], preferred_element_type=jnp.float32
        )

    @pl.when(step == steps - 1)
    def _():
        out_ref[...] = sum_ref[...].astype(out_ref.dtype)


def project(blocks, tops, tokens, features, basis, offsets):
    columns = basis.shape[1]
    deep = 256
    steps = (blocks[0].shape[1] - features) // deep
    tails = [pl.BlockSpec((x.shape[0], deep), lambda i: (0, features // deep + i)) for x in blocks]
    return pl.pallas_call(
        functools.partial(project_kernel, tops, steps),
        name="project",
        out_shape=jax.ShapeDtypeStruct((tokens, columns), basis.dtype),
        grid=(steps,),
        in_specs=[pl.BlockSpec(memory_space=pltpu.SMEM), *tails, pl.BlockSpec(basis.shape, lambda i: (0, 0))],
        out_specs=pl.BlockSpec((tokens, columns), lambda i: (0, 0)),
        scratch_shapes=[pltpu.VMEM((tokens, columns), jnp.float32)],
        compiler_params=pltpu.CompilerParams(vmem_limit_bytes=VMEM_BYTES),
    )(offsets, *blocks, basis)


RING = [(0, 1), (1, 3), (3, 2), (2, 0)]


def slots_of(row):
    before = jnp.where(row < 2, 2 - 2 * row, 7 - 2 * row)
    return row, before, 3 - row, 3 - before


def hop(x, what, back=False):
    with jax.named_scope(what):
        return lax.ppermute(x, "row", [hop[::-1] for hop in RING] if back else RING)


def swap(x, axis, what):
    with jax.named_scope(what):
        return lax.ppermute(x, axis, [(0, 1), (1, 0)])


def after(x, *others):
    return lax.optimization_barrier((x, *others))[0]


def chained(activations, gradients, q_act, basis_grad, lengths):
    tokens = activations.shape[0]
    total = 2 * lengths.shape[1]
    window = min(tokens, 256)
    half = tokens // 2
    row, core, me = lax.axis_index("row"), lax.axis_index("col"), lax.axis_index("dp")
    home = row // 2 == me
    outer = (row == 0) | (row == 3)
    spans = [lengths, swap(lengths, "dp", "lengths_dp")]
    places = [2 * x + c for x in slots_of(row) for c in (core, 1 - core)]
    turn = home == outer
    picks = [jnp.where(home, 0, 1), jnp.where(turn, 1, 0), jnp.where(turn, 0, 1)]
    place = jnp.where(home, row, 3 - row) % 2
    plan = jnp.stack([*places, *picks, place, 1 - place, core]).astype(jnp.int32)
    PICK, TURN, AGAIN, NEAR, FAR, CORE = range(8, 14)

    features = gradients.shape[1]

    def crossed(chunks, place):
        return [swap(x, "col", f"tokens_{place}_cols_{i}") for i, x in enumerate(chunks)]

    def fold(start, mine, theirs, place):
        return fold_block(start, mine, theirs, basis_grad, features, plan, place, jnp.float32)[0]

    own = [jnp.concatenate([x[i : i + half] for x in (gradients, activations)], axis=1) for i in (0, half)]
    slots = [(own, crossed(own, 0))]
    start = fold_block(None, *slots[0], basis_grad, features, plan, 0, jnp.float32, 2)

    def piece(sums, x, place, i):
        theirs = swap(x, "col", f"tokens_{place}_cols_{i}")
        kind = jnp.bfloat16 if place == 3 else jnp.float32
        return theirs, fold_block(sums, [x], [theirs], basis_grad, features, plan, place, kind)[0]

    owns, kept, sums = [None, None], [[], [], []], list(start)
    firsts = [hop(x, f"tokens_first_{i}") for i, x in enumerate(own)]
    seconds = [hop(after(x, sums[i], spans[1]), f"tokens_second_{i}") for i, x in enumerate(firsts)]
    thirds = []
    for i in range(2):
        theirs, sums[i] = piece(sums[i], firsts[i], 1, i)
        kept[0].append((firsts[i], theirs))
        thirds.append(hop(after(seconds[i], sums[i]), f"tokens_third_{i}"))
        theirs, sums[i] = piece(sums[i], seconds[i], 2, i)
        kept[1].append((seconds[i], theirs))
    for i in (1, 0):
        third = after(thirds[i], sums[i])
        theirs, owns[i] = piece(sums[i], third, 3, i)
        kept[2].append((third, theirs))
    kept[2] = kept[2][::-1]
    slots += [tuple(zip(*pairs)) for pairs in kept]

    first = [hop(x, f"rot_first_{i}", i == 1) for i, x in enumerate(owns)]
    blocks = [x for mine, theirs in slots for x in (*mine, *theirs)]
    blocks[-1] = after(blocks[-1], *owns)
    tops = [(top, 2 * place + i) for place in range(4) for i in range(2) for top in (0, half)]
    rotated = project(blocks, tops, tokens, features, q_act, plan)
    other = swap(rotated, "dp", "act_dp")
    second = [None, hop(after(first[1], owns[0]), "rot_second_1", True)]
    second[0] = hop(after(first[0], rotated), "rot_second_0")
    cross_first = swap(jnp.where(turn, first[0], first[1]), "dp", "rot_first_dp")
    early = [jnp.where(home, s, o) for s, o in zip(second, owns)]
    early[1] = swap(early[1], "dp", "rot_second_dp_1")
    third = [None, hop(second[1], "rot_third_1", True)]
    third[0] = hop(after(second[0], third[1], cross_first, early[1], other), "rot_third_0")
    early[0] = swap(early[0], "dp", "rot_second_dp_0")
    acts = [(x, swap(x, "col", "rot_act_cols")) for x in (rotated, other)]
    acts = [masked_windows(plan, CORE, s, *x, window) for s, x in zip(spans, acts)]
    cross_third = jnp.where(turn, third[1], third[0])
    cross_third = swap(after(cross_third, *early, *acts), "dp", "rot_third_dp")

    near = [[(PICK, (o, s)) for o, s in zip(owns, second)], [(PICK, (x,)) for x in early]]
    far = [[(TURN, (first[0], third[0])), (AGAIN, (first[1], third[1]))], [(at, (cross_first, cross_third)) for at in (TURN, AGAIN)]]
    out = squared_sums(plan, spans, acts, near, window, total, 2, NEAR)
    return squared_sums(plan, spans, acts, far, window, total, 2, FAR, out)


def fold_with(basis, section):
    return jnp.dot(section, basis, preferred_element_type=jnp.float32).astype(jnp.bfloat16)


def gathered(activations, gradients, q_act, basis_grad, lengths):
    n_dp = lax.axis_size("dp")
    total = lengths.shape[1] * n_dp
    window = min(activations.shape[0], 256)
    me = lax.axis_index("dp")
    plan = jnp.stack([jnp.int32(0), lax.axis_index("col").astype(jnp.int32)])

    def shifted(x, k):
        return lax.ppermute(x, "dp", [(i, (i + k) % n_dp) for i in range(n_dp)])

    rotated_g = fold_with(basis_grad, lax.all_gather(gradients, ("row", "col"), axis=1, tiled=True))
    rotated = fold_with(q_act, lax.all_gather(activations, ("row", "col"), axis=1, tiled=True))
    acts, spans = [rotated], [lengths]
    for k in range(1, n_dp):
        acts.append(shifted(rotated, k))
        spans.append(shifted(lengths, k))
    acts = [masked_windows(plan, 1, s, x, swap(x, "col", "cols"), window) for x, s in zip(acts, spans)]

    rotated_g = lax.all_gather(rotated_g, "row", axis=1, tiled=True)
    columns = rotated_g.shape[1] // n_dp

    def columns_of(d):
        return lax.dynamic_slice_in_dim(rotated_g, d % n_dp * columns, columns, axis=1)

    grads = [columns_of(me)]
    for k in range(1, n_dp):
        grads.append(shifted(columns_of(me + k), k))
    return squared_sums(plan, spans, acts, [[(0, [x])] for x in grads], window, total)


def on_device(activations, gradients, q_act, q_grad, lengths):
    basis_grad = q_grad.reshape(q_grad.shape[0], q_grad.shape[2])
    fits = lax.axis_size("row") == 4 and lax.axis_size("dp") == 2 and lax.axis_size("col") == 2
    plan = chained if fits else gathered
    return plan(activations, gradients, q_act, basis_grad, lengths)


def solution(mesh):
    return jax.shard_map(
        on_device,
        mesh=mesh,
        in_specs=(
            P(("parts", "dp"), ("row", "col")),
            P(("parts", "dp"), ("row", "col")),
            P(None, ("row", "col")),
            P(None, "col", "row"),
            P(("parts", "dp"), None),
        ),
        out_specs=P(("parts", "row"), ("col", "dp")),
        check_vma=False,
    )
```
